32 devices in a mesh: row: 8 (over y, x, core), rhs: 4 (over z).
Axes of the slice: x: 2, y: 2, z: 4, core: 2. Of those that a mesh axis runs over, the one named last changes fastest.
Arguments:
- right_sides: float32 [16384, 4096], P('row', 'rhs'), may hold values from -6 to 6
- panel_diag: float32 [2, 512, 512], replicated, as said below
- left_factor: bfloat16 [16384, 2, 512], P('row', None, 'rhs'), may hold values from -0.25 to 0.25
- right_factor: bfloat16 [16384, 2, 512], P('row', None, 'rhs'), may hold values from -0.25 to 0.25
- tile_scale: float32 [32, 2], P('row'), may hold values from 0.3 to 1.5
- tile_rank: int32 [32, 2], P('row'), may hold values from 128 to 512, as said below
Outputs:
- solved: float32 [16384, 4096], P('row', 'rhs')
The draws below stay inside these ranges and needn't reach their ends.
Inputs may be any that keep to these rules, and one draw needn't show every extreme that they name: panel_diag[k] is lower triangular with diagonal entries of 1 or more. `tile_rank`: every rank is a multiple of 128; some block has rank 512 in both panels.
All inputs are finite; a program needn't handle non-finite values.
Results may differ from the reference program's by a relative error of at most 0.0003.
Values may be sent and summed in bfloat16 or wider, within the bound.
A program may use at most 128 MiB of HBM per device.

```python
import math
import jax
import jax.numpy as jnp
from jax import lax

P_SIZE = 512
RSTEP = 128
BLK_DEV = 4
NBLK = 32
ROWS = 16384
NRHS = 4096
N_ROW = 8


def draw_panel_diag(key, part):
    first_key, second_key = jax.random.split(jax.random.fold_in(key, 11))
    lower_part = jax.random.normal(first_key, (2, P_SIZE, P_SIZE), jnp.float32) * (0.8 / math.sqrt(P_SIZE))
    middle = jax.random.uniform(second_key, (2, P_SIZE), jnp.float32, 1.0, 3.0)
    return jnp.tril(lower_part, -1) + middle[:, :, None] * jnp.eye(P_SIZE, dtype=jnp.float32)[None]


def draw_tile_rank(key, part):
    first_key, second_key = jax.random.split(jax.random.fold_in(key, 23))
    levels = jax.random.randint(first_key, (NBLK, 2), 1, P_SIZE // RSTEP + 1) * RSTEP
    chosen_block = jax.random.randint(second_key, (), 0, NBLK)
    position = jnp.arange(NBLK, dtype=jnp.int32)[:, None]
    return jnp.where(position == chosen_block, P_SIZE, levels).astype(jnp.int32)


def block_levels(rng, shape, cuts, least, largest):
    gain = 1.0
    for dim, shards_of in cuts:
        steps = jax.random.uniform(jax.random.fold_in(jax.random.fold_in(rng, 6), dim), (shards_of,), jnp.float32, least / len(cuts), largest / len(cuts))
        gain = gain * jnp.repeat(jnp.exp(steps), shape[dim] // shards_of).reshape((-1,) + (1,) * (len(shape) - 1 - dim))
    return gain


def centred(own_key, dims, deviation, most, shards=(), held_as=jnp.bfloat16):
    factor_of = block_levels(own_key, dims, shards, -0.22, 0.18) if shards else 1.0
    values = jax.random.normal(own_key, dims, jnp.float32) * deviation * factor_of
    return jnp.minimum(jnp.maximum(values, -most), most).astype(held_as)


def setup_inputs(seed: int = 0) -> dict:
    splits = jax.random.split(jax.random.key(seed), 7)
    right_sides = centred(splits[0], (ROWS, NRHS), 1.0, 6.0, ((0, 8), (1, 4)), jnp.float32)
    panel_diag = draw_panel_diag(jax.random.fold_in(splits[6], 71), 0)
    left_factor = centred(splits[2], (ROWS, 2, P_SIZE), P_SIZE ** -0.5, 0.25, ((0, 8), (2, 4)))
    right_factor = centred(splits[3], (ROWS, 2, P_SIZE), P_SIZE ** -0.5, 0.25, ((0, 8), (2, 4)))
    tile_scale = jnp.clip(jnp.exp(math.log(1.5) - 1.60943787 * jax.random.uniform(splits[4], (NBLK, 2), jnp.float32) ** block_levels(splits[4], (NBLK, 2), ((0, 8),), -0.2, 0.2)), 0.3, 1.5)
    tile_rank = draw_tile_rank(jax.random.fold_in(splits[6], 71), 0)
    return {"right_sides": right_sides, "panel_diag": panel_diag, "left_factor": left_factor, "right_factor": right_factor, "tile_scale": tile_scale, "tile_rank": tile_rank}


def reference(right_sides, panel_diag, left_factor, right_factor, tile_scale, tile_rank):
    blocks = right_sides.reshape(N_ROW, BLK_DEV, P_SIZE, NRHS)
    left_all = left_factor.reshape(N_ROW, BLK_DEV, P_SIZE, 2, P_SIZE)
    right_all = right_factor.reshape(N_ROW, BLK_DEV, P_SIZE, 2, P_SIZE)
    scales = tile_scale.reshape(N_ROW, BLK_DEV, 2)
    ranks = tile_rank.reshape(N_ROW, BLK_DEV, 2)
    global_block = (jnp.arange(BLK_DEV, dtype=jnp.int32)[None, :] * N_ROW + jnp.arange(N_ROW, dtype=jnp.int32)[:, None]).astype(jnp.int32)
    columns = jnp.arange(P_SIZE, dtype=jnp.int32)
    for panel_index in range(2):
        solution = lax.linalg.triangular_solve(panel_diag[panel_index], blocks[panel_index, 0], left_side=True, lower=True)

        def update(items):
            left_block, right_block, scale_row, rank_row, global_row, target = items
            weight = jnp.where(global_row > panel_index, scale_row, 0.0).astype(jnp.float32)[:, None] * (columns[None, :] < rank_row[:, None]).astype(jnp.float32)
            inner = jnp.einsum('lqr,qn->lrn', right_block[:, :, panel_index, :].astype(jnp.float32), solution, precision=lax.Precision.HIGHEST)
            inner = inner * weight[:, :, None]
            return target - jnp.einsum('lpr,lrn->lpn', left_block[:, :, panel_index, :].astype(jnp.float32), inner, precision=lax.Precision.HIGHEST)
        blocks = lax.map(update, (left_all, right_all, scales[:, :, panel_index], ranks[:, :, panel_index], global_block, blocks))
        blocks = blocks.at[panel_index, 0].set(solution)
    return blocks.reshape(ROWS, NRHS)
```

```python
import functools

import jax
import jax.numpy as jnp
from jax import lax
from jax.experimental import pallas as pl
from jax.experimental.pallas import tpu as pltpu
from jax.sharding import PartitionSpec as P

MESH = pl.DeviceIdType.MESH
HIGHEST = lax.Precision.HIGHEST
BASE = 128


def split(value):
    high = value.astype(jnp.bfloat16)
    return high, (value - high.astype(jnp.float32)).astype(jnp.bfloat16)


def dot(a, b, precision=None):
    return jnp.dot(a, b, preferred_element_type=jnp.float32, precision=precision)


def invert_lower(block):
    size = block.shape[0]
    row = lax.broadcasted_iota(jnp.int32, block.shape, 0)
    column = lax.broadcasted_iota(jnp.int32, block.shape, 1)
    inverse = jnp.where(row == column, 1.0 / jnp.where(row == column, block, 1.0), 0.0)
    width = 1
    while width < size:
        row_part, column_part = row // width, column // width
        coupling = jnp.where(
            (row_part % 2 == 1) & (row_part - 1 == column_part), block, 0.0
        )
        inverse = inverse - dot(inverse, dot(coupling, inverse, HIGHEST), HIGHEST)
        width *= 2
    return inverse


def front_kernel(
    rows, ranks,
    scale, sides, diag, factors, out,
    gathered, held, high, low, solved, inverse,
    own_sem, in_sem, out_sem, send_sem, recv_sem, x_send, x_recv,
):
    row, rank = lax.axis_index("row"), lax.axis_index("rhs")
    tiles = factors.shape[0]
    blocks = tiles // 2
    size = diag.shape[1]
    chunks, chunk = solved.shape[1], solved.shape[4]
    bits = rows.bit_length() - 1

    own_copy = pltpu.make_async_copy(factors, gathered.at[rank], own_sem)
    loads = [
        pltpu.make_async_copy(sides.at[l], held.at[l], in_sem.at[l]) for l in range(blocks)
    ]
    stores = [
        pltpu.make_async_copy(held.at[l], out.at[l], out_sem.at[l]) for l in range(blocks)
    ]
    for load in loads:
        load.start()
    own_copy.start()

    barrier = pltpu.get_barrier_semaphore()
    for step in (1, ranks - 1):
        pl.semaphore_signal(
            barrier, inc=1, device_id=(row, lax.rem(rank + step, ranks)), device_id_type=MESH
        )
    for bit in range(bits):
        pl.semaphore_signal(
            barrier, inc=1, device_id=(row ^ (1 << bit), rank), device_id_type=MESH
        )
    pl.semaphore_wait(barrier, 2 + bits)

    def relay(side, tile, hop, own=False):
        step = 1 if side == 0 else -1
        origin = lax.rem(rank - step * hop + 2 * ranks, ranks)
        target = lax.rem(rank + step + ranks, ranks)
        return pltpu.make_async_remote_copy(
            src_ref=factors.at[tile] if hop == 0 else gathered.at[origin, tile],
            dst_ref=gathered.at[origin, tile],
            send_sem=send_sem.at[side, tile, hop],
            recv_sem=recv_sem.at[side, tile, hop],
            device_id=(row, target),
            device_id_type=MESH,
        )

    def sends(side, hop):
        if side == 0:
            return (rank >= hop) & (rank + 1 < ranks)
        return (rank + hop < ranks) & (rank >= 1)

    def receives(side, hop):
        return rank >= hop + 1 if side == 0 else rank + hop + 1 < ranks

    def start_relay(side, tile, hop):
        @pl.when(sends(side, hop))
        def _():
            relay(side, tile, hop).start()

    def wait_relay(side, tile, hop):
        @pl.when(receives(side, hop))
        def _():
            relay(side, tile, hop).wait_recv()

    def pass_on(panel, part, bit):
        return pltpu.make_async_remote_copy(
            src_ref=solved.at[panel, part],
            dst_ref=solved.at[panel, part],
            send_sem=x_send.at[panel, part, bit],
            recv_sem=x_recv.at[panel, part],
            device_id=(row ^ (1 << bit), rank),
            device_id_type=MESH,
        )

    def pass_down(panel, part, start=True):
        relative = row ^ panel
        for bit in range(bits):
            @pl.when(lax.rem(relative, 2 << bit) == 0)
            def _():
                copy = pass_on(panel, part, bit)
                if start:
                    copy.start()
                else:
                    copy.wait_send()

    def take_solution(panel):
        @pl.when(row != panel)
        def _():
            for part in range(chunks):
                pass_on(panel, part, 0).wait_recv()
                pass_down(panel, part)

    def product(tile, panel, part):
        a, b = high[tile], low[tile]
        x, y = solved[panel, part, 0], solved[panel, part, 1]
        return dot(a, x) + (dot(b, x) + dot(a, y))

    def prepare(panel):
        for i in range(size // BASE):
            span = pl.ds(i * BASE, BASE)
            inverse[i] = invert_lower(diag[panel, span, span])

    def solve(panel):
        for part in range(chunks):
            columns = pl.ds(part * chunk, chunk)
            for i in range(size // BASE):
                span = pl.ds(i * BASE, BASE)
                value = held[0, span, columns]
                if i:
                    value = value - dot(
                        diag[panel, span, pl.ds(0, i * BASE)],
                        held[0, pl.ds(0, i * BASE), columns],
                        HIGHEST,
                    )
                value = dot(inverse[i], value, HIGHEST)
                held[0, span, columns] = value
                top, rest = split(value)
                solved[panel, part, 0, span, :] = top
                solved[panel, part, 1, span, :] = rest
            pass_down(panel, part)

    def form(tile):
        total = None
        for origin in range(ranks):
            term = lax.dot_general(
                gathered[origin, tile, 0],
                gathered[origin, tile, 1],
                (((1,), (1,)), ((), ())),
                preferred_element_type=jnp.float32,
            )
            total = term if total is None else total + term
        top, rest = split(total * scale[tile // 2, tile % 2])
        high[tile], low[tile] = top, rest

    def update(block):
        @pl.loop(0, chunks)
        def _(part):
            columns = pl.ds(pl.multiple_of(part * chunk, chunk), chunk)
            held[block, :, columns] = held[block, :, columns] - (
                product(2 * block, 0, part) + product(2 * block + 1, 1, part)
            )

    for tile in range(min(2, tiles)):
        for side in range(2):
            start_relay(side, tile, 0)

    @pl.when(row < 2)
    def _():
        prepare(row)

    loads[0].wait()

    @pl.when(row == 0)
    def _():
        solve(0)

    own_copy.wait()
    done = 0
    for slot in range(1, tiles + ranks - 1):
        for hop in range(ranks - 2, 0, -1):
            tile = slot - hop
            if 0 <= tile < tiles:
                for side in range(2):
                    wait_relay(side, tile, hop - 1)
                    start_relay(side, tile, hop)
        if slot + 1 < tiles:
            for side in range(2):
                start_relay(side, slot + 1, 0)
        tile = slot - (ranks - 1)
        if tile >= 0:
            for side in range(2):
                wait_relay(side, tile, ranks - 2)
            form(tile)
        if slot == ranks - 2:
            take_solution(0)
        if slot == ranks - 1:

            @pl.when(row == 1)
            def _():
                @pl.loop(0, chunks)
                def _(part):
                    columns = pl.ds(pl.multiple_of(part * chunk, chunk), chunk)
                    held[0, :, columns] = held[0, :, columns] - product(0, 0, part)

                solve(1)

        if slot == ranks + 1:
            take_solution(1)
        while slot >= ranks + 1 and done < blocks and 2 * done + 1 <= tile:
            if done == 0:

                @pl.when(row >= 2)
                def _():
                    update(0)

            else:
                loads[done].wait()
                update(done)
            stores[done].start()
            done += 1

    for side in range(2):
        for tile in range(tiles):
            for hop in range(ranks - 1):
                @pl.when(sends(side, hop))
                def _():
                    relay(side, tile, hop).wait_send()

    for panel in range(2):
        for part in range(chunks):
            pass_down(panel, part, start=False)
    for store in stores:
        store.wait()


def shards(right_sides, panel_diag, left_factor, right_factor, tile_scale, tile_rank):
    row_count, column_count = right_sides.shape
    size = panel_diag.shape[1]
    blocks = row_count // size
    tiles = 2 * blocks
    rows, ranks = lax.axis_size("row"), lax.axis_size("rhs")
    width = left_factor.shape[2]
    global_block = jnp.arange(blocks, dtype=jnp.int32) * rows + lax.axis_index("row")
    scale = jnp.where(
        global_block[:, None] > jnp.arange(2, dtype=jnp.int32)[None], tile_scale, 0.0
    )
    column = lax.axis_index("rhs") * width + jnp.arange(width, dtype=jnp.int32)
    used = column[None, None, None, :] < tile_rank[:, None, :, None]
    left = left_factor.reshape(blocks, size, 2, width)
    left = jnp.where(used, left, jnp.zeros((), left.dtype))
    right = right_factor.reshape(blocks, size, 2, width)
    factors = jnp.stack([left, right], axis=0).transpose(1, 3, 0, 2, 4)
    factors = factors.reshape(tiles, 2, size, width)
    chunk = min(256, column_count)
    chunks = column_count // chunk
    bits = rows.bit_length() - 1
    hops = ranks - 1
    out = pl.pallas_call(
        functools.partial(front_kernel, rows, ranks),
        out_shape=jax.ShapeDtypeStruct((blocks, size, column_count), jnp.float32),
        in_specs=[
            pl.BlockSpec(memory_space=pltpu.SMEM),
            pl.BlockSpec(memory_space=pl.ANY),
            pl.BlockSpec(memory_space=pltpu.VMEM),
            pl.BlockSpec(memory_space=pl.ANY),
        ],
        out_specs=pl.BlockSpec(memory_space=pl.ANY),
        scratch_shapes=[
            pltpu.VMEM((ranks, tiles, 2, size, width), jnp.bfloat16),
            pltpu.VMEM((blocks, size, column_count), jnp.float32),
            pltpu.VMEM((tiles, size, size), jnp.bfloat16),
            pltpu.VMEM((tiles, size, size), jnp.bfloat16),
            pltpu.VMEM((2, chunks, 2, size, chunk), jnp.bfloat16),
            pltpu.VMEM((size // BASE, BASE, BASE), jnp.float32),
            pltpu.SemaphoreType.DMA,
            pltpu.SemaphoreType.DMA((blocks,)),
            pltpu.SemaphoreType.DMA((blocks,)),
            pltpu.SemaphoreType.DMA((2, tiles, hops)),
            pltpu.SemaphoreType.DMA((2, tiles, hops)),
            pltpu.SemaphoreType.DMA((2, chunks, bits)),
            pltpu.SemaphoreType.DMA((2, chunks)),
        ],
        compiler_params=pltpu.CompilerParams(
            collective_id=0, has_side_effects=True, vmem_limit_bytes=60 * 1024 * 1024
        ),
    )(scale, right_sides.reshape(blocks, size, column_count), panel_diag, factors)
    return out.reshape(row_count, column_count)


def solution(mesh):
    placed = (
        P("row", "rhs"),
        P(),
        P("row", None, "rhs"),
        P("row", None, "rhs"),
        P("row", None),
        P("row", None),
    )
    return jax.shard_map(
        shards, mesh=mesh, in_specs=placed, out_specs=P("row", "rhs"), check_vma=False
    )
```
